256 devices in a mesh: dp: 8 (over y, z_lo), seq: 32 (over x, z_hi, core).
Axes of the slice: x: 4, y: 4, z: 8 (z_hi: 4, z_lo: 2; z = z_hi * 2 + z_lo), core: 2. Of those that a mesh axis runs over, the one named last changes fastest.
Arguments:
- queries: bfloat16 [32768, 1024], P(('dp', 'seq')), parts along dimension 0, may hold values from -8 to 8
- key_rows: bfloat16 [32768, 1024], P(('dp', 'seq')), parts along dimension 0, may hold values from -8 to 8
- value_rows: bfloat16 [32768, 1024], P(('dp', 'seq')), parts along dimension 0, may hold values from -6 to 6
- out_cotangent: bfloat16 [32768, 1024], P(('dp', 'seq')), parts along dimension 0, may hold values from -6 to 6
- scale_starts: int32 [96], P('dp'), parts along dimension 0, may hold values from 0 to 1031, as said below
Outputs:
- attended: bfloat16 [32768, 1024], P(('dp', 'seq')), parts along dimension 0
- query_grad: bfloat16 [32768, 1024], P(('dp', 'seq')), parts along dimension 0
- key_grad: bfloat16 [32768, 1024], P(('dp', 'seq')), parts along dimension 0
- value_grad: bfloat16 [32768, 1024], P(('dp', 'seq')), parts along dimension 0
The draws below stay inside these ranges and needn't reach their ends.
There are 8 independent parts, one for each index of `dp`. The reference program is written for one: setup_inputs(seed, part) draws one part's arguments, and reference() takes and returns one part's arrays. A program takes and returns all parts, laid end to end along the dimension named above; each array names one. Nothing has to cross between parts.
Inputs may be any that keep to these rules, and one draw needn't show every extreme that they name: `scale_starts`: the first token of each of the 12 scales in order: the first is 0, each is larger than the one before, all lie below 4096.
All inputs are finite; a program needn't handle non-finite values.
Results may differ from the reference program's by a relative error of at most 0.011.
Values may be sent and summed in bfloat16 or wider, within the bound.
A program may use at most 128 MiB of HBM per device.

```python
import math
import jax
import jax.numpy as jnp
from jax import lax

HEADS = 8
HEAD_DIM = 128
WIDTH = 1024
SCALES = 12
TOK_DEV = 128
TOKENS = 4096
N_SEQ = 32


def draw_queries(key, part):
    key = jax.random.fold_in(key, 1)
    values = jnp.clip(jax.random.normal(key, (TOKENS, WIDTH), jnp.float32), -6.0, 6.0)
    return values.astype(jnp.bfloat16)


def draw_key_rows(key, part):
    key = jax.random.fold_in(key, 2)
    values = jnp.clip(jax.random.normal(key, (TOKENS, WIDTH), jnp.float32), -6.0, 6.0)
    return values.astype(jnp.bfloat16)


def draw_scale_starts(key, part):
    key = jax.random.fold_in(key, 3)
    spread = TOKENS - SCALES
    summit = 4 ** (SCALES - 1)
    base = jnp.array([section + spread * 4 ** section // (5 * summit) for section in range(SCALES)], dtype=jnp.int32)
    jitter_cap = jnp.array([1 + spread * 4 ** section // (20 * summit) for section in range(SCALES)], dtype=jnp.int32)
    section_index = jnp.arange(SCALES, dtype=jnp.int32)
    jitter = jax.random.randint(key, (SCALES,), 0, jitter_cap)
    jitter = jnp.where(section_index == SCALES - 1, jitter_cap - 1, jitter)
    return (base + jitter).astype(jnp.int32)


def block_levels(rng, dims, split, least, high):
    def one(position, parts):
        draws = jax.random.uniform(jax.random.fold_in(jax.random.fold_in(rng, 6), position), (parts,), jnp.float32, least / len(split), high / len(split))
        return jnp.repeat(jnp.exp(draws), dims[position] // parts).reshape((-1,) + (1,) * (len(dims) - position - 1))

    gain = one(*split[0])
    for cut in split[1:]:
        gain = gain * one(*cut)
    return gain


def normal_values(rng, extent, deviation, reach, shards=(), kind=jnp.bfloat16):
    drawn = jax.random.normal(rng, extent, jnp.float32) * deviation
    if len(shards) > 0:
        drawn = block_levels(rng, extent, shards, -0.22, 0.18) * drawn
    return jnp.clip(drawn, min=-reach, max=reach).astype(kind)


def setup_inputs(seed: int = 0, part: int = 0) -> dict:
    key_of = jax.random.split(jax.random.key(seed), 6)
    part_splits = jax.random.split(jax.random.fold_in(key_of[5], part), 6)
    return {
        "queries": draw_queries(jax.random.fold_in(jax.random.fold_in(key_of[5], part), 71), part),
        "key_rows": draw_key_rows(jax.random.fold_in(jax.random.fold_in(key_of[5], part), 71), part),
        "value_rows": normal_values(part_splits[2], (TOKENS, WIDTH), 1.0, 6.0, ((0, 32),)),
        "out_cotangent": normal_values(part_splits[3], (TOKENS, WIDTH), 1.0, 6.0, ((0, 32),)),
        "scale_starts": draw_scale_starts(jax.random.fold_in(jax.random.fold_in(key_of[5], part), 71), part),
    }


NEG_LARGE = -1e+30

def scale_index(positions, scale_starts):
    reached = (positions[:, None] >= scale_starts[None, :]).astype(jnp.int32)
    return (lax.optimization_barrier(jnp.sum(reached, axis=1)) - 1).astype(jnp.int32)

def rounded(array):
    return lax.optimization_barrier(array.astype(jnp.bfloat16)).astype(jnp.float32)

def reference(queries, key_rows, value_rows, out_cotangent, scale_starts):
    factor = 1.0 / math.sqrt(HEAD_DIM)
    highest = lax.Precision.HIGHEST
    keys_wide = key_rows.astype(jnp.float32).reshape(TOKENS, HEADS, HEAD_DIM)
    values_wide = value_rows.astype(jnp.float32).reshape(TOKENS, HEADS, HEAD_DIM)
    key_scale = scale_index(jnp.arange(TOKENS, dtype=jnp.int32), scale_starts)
    query_blocks = queries.reshape(N_SEQ, TOK_DEV, HEADS, HEAD_DIM)
    cotangent_blocks = out_cotangent.reshape(N_SEQ, TOK_DEV, HEADS, HEAD_DIM)
    block_numbers = jnp.arange(N_SEQ, dtype=jnp.int32)

    def block_step(carried, inputs):
        key_sum, value_sum = carried
        query_block, cotangent_block, block_number = inputs
        positions = block_number * TOK_DEV + jnp.arange(TOK_DEV, dtype=jnp.int32)
        visible = key_scale[None, :] <= scale_index(positions, scale_starts)[:, None]
        query_wide = query_block.astype(jnp.float32)
        cotangent_wide = cotangent_block.astype(jnp.float32)
        scores = jnp.einsum('qhd,khd->hqk', query_wide, keys_wide, precision=highest) * factor
        masked = jnp.where(visible[None], scores, NEG_LARGE)
        row_max = lax.optimization_barrier(jnp.max(masked, axis=2, keepdims=True))
        row_total = lax.optimization_barrier(jnp.sum(jnp.exp(masked - row_max), axis=2, keepdims=True))
        log_norm = row_max + jnp.log(row_total)
        weights = jnp.exp(masked - log_norm)
        prob_half = rounded(weights)
        attended = jnp.einsum('hqk,khd->qhd', prob_half, values_wide, precision=highest).astype(jnp.bfloat16)
        prob_grad = jnp.einsum('qhd,khd->hqk', cotangent_wide, values_wide, precision=highest)
        inner_sum = lax.optimization_barrier(jnp.sum(weights * prob_grad, axis=2))
        mixed_half = rounded(weights * prob_grad)
        mixed_part = jnp.einsum('hqk,khd->hqd', mixed_half, keys_wide, precision=highest)
        key_part = jnp.einsum('hqk,khd->hqd', prob_half, keys_wide, precision=highest)
        query_total = (mixed_part - inner_sum[:, :, None] * key_part) * factor
        query_grad = jnp.transpose(query_total, (1, 0, 2)).astype(jnp.bfloat16)
        score_grad = weights * (prob_grad - inner_sum[:, :, None])
        score_half = rounded(score_grad)
        key_sum = key_sum + jnp.einsum('hqk,qhd->khd', score_half, query_wide, precision=highest)
        value_sum = value_sum + jnp.einsum('hqk,qhd->khd', prob_half, cotangent_wide, precision=highest)
        return ((key_sum, value_sum), (attended.reshape(TOK_DEV, WIDTH), query_grad.reshape(TOK_DEV, WIDTH)))
    zeros_init = jnp.zeros((TOKENS, HEADS, HEAD_DIM), jnp.float32)
    totals, stacked = lax.scan(block_step, (zeros_init, zeros_init), (query_blocks, cotangent_blocks, block_numbers))
    key_sum, value_sum = totals
    attended, query_grad = stacked
    key_grad = (key_sum * factor).reshape(TOKENS, WIDTH).astype(jnp.bfloat16)
    value_grad = value_sum.reshape(TOKENS, WIDTH).astype(jnp.bfloat16)
    return (attended.reshape(TOKENS, WIDTH), query_grad.reshape(TOKENS, WIDTH), key_grad, value_grad)
```

```python
import functools
import math

import jax
import jax.numpy as jnp
from jax import lax
from jax.experimental import pallas as pl
from jax.experimental.pallas import tpu as pltpu
from jax.sharding import PartitionSpec as P

HEADS = 8
D = 128
TOK = 128
NX = 4
NZ = 4
COL = NZ * 2 * TOK
TOKENS = NX * COL
SCALES = 12
FACTOR = 1.0 / math.sqrt(D)
EXP2_FACTOR = FACTOR * math.log2(math.e)
NEG = -1e30
BIG = 1 << 30
MESH = pl.DeviceIdType.MESH
F32 = jnp.float32
BF16 = jnp.bfloat16
PARTNERS = (4, 5, 2, 3, 6, 7, 1)


def coords():
    s = lax.axis_index("seq")
    return s // 8, (s // 2) % 4, s % 2


def device(x, z, c):
    return (lax.axis_index("dp"), lax.rem(x, NX) * 8 + lax.rem(z, NZ) * 2 + lax.rem(c, 2))


def rows_of(start, size):
    return pl.ds(pl.multiple_of(start, TOK), size)


def dot(a, b):
    return jnp.dot(a, b, preferred_element_type=F32)


def barrier(x, z, c):
    sem = pltpu.get_barrier_semaphore()
    for i in PARTNERS:
        pl.semaphore_signal(sem, inc=1, device_id=device(x, z + i // 2, c + i % 2), device_id_type=MESH)
    for dx in (1, 3):
        pl.semaphore_signal(sem, inc=1, device_id=device(x + dx, z, c), device_id_type=MESH)
    pl.semaphore_wait(sem, len(PARTNERS) + 2)


def gather_kernel(q_ref, k_ref, v_ref, g_ref, qo, ko, vo, go, zs, zr, loc, xs, xr):
    x, z, c = coords()
    me = z * 2 + c
    barrier(x, z, c)
    base = x * COL
    plan = ((k_ref, ko, base), (v_ref, vo, base), (q_ref, qo, 0), (g_ref, go, 0))

    def z_copy(a, i):
        src, dst, off = plan[a]
        pz, pc = lax.rem(z + i // 2, NZ), lax.rem(c + i % 2, 2)
        there = dst.at[rows_of(off + me * TOK, TOK)]
        mine = src.at[:, pl.ds(pl.multiple_of((pz * 2 + pc) * D, D), D)]
        if i == 0:
            return pltpu.make_async_copy(mine, there, loc.at[a])
        return pltpu.make_async_remote_copy(
            src_ref=mine, dst_ref=there, send_sem=zs.at[a, i], recv_sem=zr.at[a, i],
            device_id=device(x, pz, pc), device_id_type=MESH,
        )

    zc = [[z_copy(a, i) for i in (0,) + PARTNERS] for a in range(4)]
    for copies in zc:
        for copy in copies:
            copy.start()

    HALF = COL // 2

    def x_copy(a, kind, dx, col, half):
        ref = (ko, vo)[a].at[rows_of(lax.rem(col, NX) * COL + half * HALF, HALF)]
        return pltpu.make_async_remote_copy(
            src_ref=ref, dst_ref=ref, send_sem=xs.at[a, kind], recv_sem=xr.at[a, kind],
            device_id=device(x + dx, z, c), device_id_type=MESH,
        )

    xc = []
    for a in range(2):
        for copy in zc[a]:
            copy.wait() if copy is zc[a][0] else copy.wait_recv()
        own = [x_copy(a, 0, 1, x, 0), x_copy(a, 1, 3, x, 1), x_copy(a, 2, 1, x, 1), x_copy(a, 3, 3, x, 0)]
        for copy in own:
            copy.start()
        xc.append(own)
    for a in range(2):
        own = xc[a]
        own[0].wait_recv()
        f0 = x_copy(a, 4, 1, x + 3, 0)
        f0.start()
        own[1].wait_recv()
        f1 = x_copy(a, 5, 3, x + 1, 1)
        f1.start()
        own += [f0, f1]
    for a in range(2):
        for n, copy in enumerate(xc[a]):
            if n >= 2:
                copy.wait_recv()
            copy.wait_send()
    for a in range(4):
        for copy in zc[a][1:]:
            if a >= 2:
                copy.wait_recv()
            copy.wait_send()
    for a in (2, 3):
        zc[a][0].wait()


def gather(q, k, v, g):
    small = jax.ShapeDtypeStruct((COL, D), BF16)
    large = jax.ShapeDtypeStruct((TOKENS, D), BF16)
    anyspace = pl.BlockSpec(memory_space=pl.ANY)
    return pl.pallas_call(
        gather_kernel,
        out_shape=(small, large, large, small),
        in_specs=[anyspace] * 4,
        out_specs=[anyspace] * 4,
        scratch_shapes=[
            pltpu.SemaphoreType.DMA((4, 8)),
            pltpu.SemaphoreType.DMA((4, 8)),
            pltpu.SemaphoreType.DMA((4,)),
            pltpu.SemaphoreType.DMA((2, 6)),
            pltpu.SemaphoreType.DMA((2, 6)),
        ],
        compiler_params=pltpu.CompilerParams(collective_id=0, has_side_effects=True),
        name="gather",
    )(q, k, v, g)


QB = 256
KB = 256


def attention_kernel(starts, q_ref, k_ref, v_ref, g_ref, o_ref, dq_ref, dk_ref, dv_ref,
                     qt, gt, kt, vt, pt, ot, ms, ls, gs, shr, ins, dqt):
    x, _, _ = coords()
    qt[:D, :] = q_ref[...].T
    gt[...] = g_ref[...].T
    for j in range(NX):
        rows = slice(j * COL, (j + 1) * COL)
        kt[:, rows] = k_ref[rows, :].T
        vt[:, rows] = v_ref[rows, :].T
    sub = lax.broadcasted_iota(jnp.int32, (D, COL), 0)
    pos = x * COL + lax.broadcasted_iota(jnp.int32, (D, COL), 1)
    nxt = jnp.full((D, COL), BIG, jnp.int32)
    now = jnp.full((D, COL), BIG, jnp.int32)
    lane = lax.broadcasted_iota(jnp.int32, (1, D), 1)
    starts_row = jnp.full((1, D), BIG, jnp.int32)
    for s in range(SCALES):
        nxt = jnp.where(sub == s, starts[s], nxt)
        now = jnp.where(sub == s + 1, starts[s], now)
        starts_row = jnp.where(lane == s, starts[s], starts_row)
    qt[D:, :] = jnp.where((nxt > pos) & (now <= pos), NEG, 0.0).astype(BF16)

    def scores(j, b):
        rows = pl.ds(pl.multiple_of(j * COL, COL), COL)
        cols = pl.ds(pl.multiple_of(b * QB, QB), QB)
        key_pos = j * COL + lax.broadcasted_iota(jnp.int32, (COL, D), 0)
        reached = jnp.where(key_pos >= starts_row, 1.0, 0.0).astype(BF16)
        s = dot(jnp.concatenate([k_ref[rows, :], reached], axis=1), qt[:, cols])
        m = jnp.max(s, axis=0, keepdims=True)
        p = jnp.exp2(s * EXP2_FACTOR - m * EXP2_FACTOR)
        ms[j, :, cols] = m * EXP2_FACTOR
        ls[j, :, cols] = jnp.sum(p, axis=0, keepdims=True)
        half = p.astype(BF16)
        pt[rows, cols] = half
        ot[j, :, cols] = dot(vt[:, rows], half)

    def first(n, carry):
        scores(n // (COL // QB), lax.rem(n, COL // QB))
        return carry

    lax.fori_loop(0, NX * (COL // QB), first, 0)

    top = jnp.maximum(jnp.maximum(ms[0], ms[1]), jnp.maximum(ms[2], ms[3]))
    shares = [jnp.exp2(ms[j] - top) for j in range(NX)]
    total = shares[0] * ls[0] + shares[1] * ls[1] + shares[2] * ls[2] + shares[3] * ls[3]
    inverse = 1.0 / total
    shares = [share * inverse for share in shares]
    o = ot[0] * shares[0] + ot[1] * shares[1] + ot[2] * shares[2] + ot[3] * shares[3]
    o_ref[...] = o.T.astype(BF16)
    g = gt[...].astype(F32)
    inner = jnp.sum(o * g, axis=0, keepdims=True)
    for j in range(NX):
        gs[j] = (g * shares[j]).T.astype(BF16)
        shr[j] = shares[j]
    ins[...] = inner
    dqt[...] = jnp.zeros_like(dqt)

    def second(n, carry):
        j = n // (COL // KB)
        rows = pl.ds(pl.multiple_of(n * KB, KB), KB)
        p = pt[rows, :]
        dp = dot(v_ref[rows, :], gt[...])
        ds = (p.astype(F32) * shr[j] * (dp - ins[...])).astype(BF16)
        dk_ref[rows, :] = (dot(ds, q_ref[...]) * FACTOR).astype(BF16)
        dv_ref[rows, :] = dot(p, gs[j]).astype(BF16)
        dqt[...] += dot(kt[:, rows], ds)
        return carry

    lax.fori_loop(0, TOKENS // KB, second, 0)
    dq_ref[...] = (dqt[...] * FACTOR).T.astype(BF16)


def attention(starts, q, k, v, g):
    small = jax.ShapeDtypeStruct((COL, D), BF16)
    large = jax.ShapeDtypeStruct((TOKENS, D), BF16)
    vm = pl.BlockSpec(memory_space=pltpu.VMEM)
    return pl.pallas_call(
        attention_kernel,
        out_shape=(small, small, large, large),
        in_specs=[pl.BlockSpec(memory_space=pltpu.SMEM)] + [vm] * 4,
        out_specs=[vm] * 4,
        scratch_shapes=[
            pltpu.VMEM((2 * D, COL), BF16),
            pltpu.VMEM((D, COL), BF16),
            pltpu.VMEM((D, TOKENS), BF16),
            pltpu.VMEM((D, TOKENS), BF16),
            pltpu.VMEM((TOKENS, COL), BF16),
            pltpu.VMEM((NX, D, COL), F32),
            pltpu.VMEM((NX, 1, COL), F32),
            pltpu.VMEM((NX, 1, COL), F32),
            pltpu.VMEM((NX, COL, D), BF16),
            pltpu.VMEM((NX, 1, COL), F32),
            pltpu.VMEM((1, COL), F32),
            pltpu.VMEM((D, COL), F32),
        ],
        compiler_params=pltpu.CompilerParams(vmem_limit_bytes=56 * 1024 * 1024),
        name="attention",
    )(starts, q, k, v, g)


def scatter_kernel(o_ref, dq_ref, dk_ref, dv_ref, oo, dqo, dko, dvo, land, mid, red, zs, zr, loc, xs, xr):
    x, z, c = coords()
    me = z * 2 + c
    barrier(x, z, c)
    HALF = COL // 2
    parts = (dk_ref, dv_ref)

    def x_copy(a, kind, dx, src, slot):
        return pltpu.make_async_remote_copy(
            src_ref=src, dst_ref=land.at[a, slot], send_sem=xs.at[a, kind], recv_sem=xr.at[a, kind],
            device_id=device(x + dx, z, c), device_id_type=MESH,
        )

    def part(a, col, half):
        return parts[a].at[rows_of(lax.rem(col, NX) * COL + half * HALF, HALF)]

    xc = []
    for a in range(2):
        own = [
            x_copy(a, 0, 1, part(a, x + 2, 0), 0),
            x_copy(a, 1, 3, part(a, x + 2, 1), 1),
            x_copy(a, 2, 1, part(a, x + 1, 1), 2),
            x_copy(a, 3, 3, part(a, x + 3, 0), 3),
        ]
        for copy in own:
            copy.start()
        xc.append(own)

    def z_copy(a, i):
        src = (o_ref, dq_ref, red.at[0], red.at[1])[a]
        dst = (oo, dqo, dko, dvo)[a]
        pz, pc = lax.rem(z + i // 2, NZ), lax.rem(c + i % 2, 2)
        there = dst.at[:, pl.ds(pl.multiple_of(me * D, D), D)]
        mine = src.at[rows_of((pz * 2 + pc) * TOK, TOK)]
        if i == 0:
            return pltpu.make_async_copy(mine, there, loc.at[a])
        return pltpu.make_async_remote_copy(
            src_ref=mine, dst_ref=there, send_sem=zs.at[a, i], recv_sem=zr.at[a, i],
            device_id=device(x, pz, pc), device_id_type=MESH,
        )

    zc = [[z_copy(a, i) for i in (0,) + PARTNERS] for a in range(4)]
    for copies in zc[:2]:
        for copy in copies:
            copy.start()
    for a in range(2):
        own = xc[a]
        own[0].wait_recv()
        mid[a, 0] = (land[a, 0].astype(F32) + part(a, x + 1, 0)[...].astype(F32)).astype(BF16)
        f0 = x_copy(a, 4, 1, mid.at[a, 0], 4)
        f0.start()
        own[1].wait_recv()
        mid[a, 1] = (land[a, 1].astype(F32) + part(a, x + 3, 1)[...].astype(F32)).astype(BF16)
        f1 = x_copy(a, 5, 3, mid.at[a, 1], 5)
        f1.start()
        own += [f0, f1]
    for a in range(2):
        own = xc[a]
        for copy in own[2:]:
            copy.wait_recv()
        red[a, :HALF] = (
            part(a, x, 0)[...].astype(F32) + land[a, 4].astype(F32) + land[a, 3].astype(F32)
        ).astype(BF16)
        red[a, HALF:] = (
            part(a, x, 1)[...].astype(F32) + land[a, 5].astype(F32) + land[a, 2].astype(F32)
        ).astype(BF16)
        for copy in zc[2 + a]:
            copy.start()
    for a in range(2):
        for copy in xc[a]:
            copy.wait_send()
    for copies in zc:
        for copy in copies:
            copy.wait()


def scatter(o, dq, dk, dv):
    out = jax.ShapeDtypeStruct((TOK, HEADS * D), BF16)
    anyspace = pl.BlockSpec(memory_space=pl.ANY)
    vm = pl.BlockSpec(memory_space=pltpu.VMEM)
    return pl.pallas_call(
        scatter_kernel,
        out_shape=(out,) * 4,
        in_specs=[anyspace, anyspace, vm, vm],
        out_specs=[anyspace] * 4,
        scratch_shapes=[
            pltpu.VMEM((2, 6, COL // 2, D), BF16),
            pltpu.VMEM((2, 2, COL // 2, D), BF16),
            pltpu.VMEM((2, COL, D), BF16),
            pltpu.SemaphoreType.DMA((4, 8)),
            pltpu.SemaphoreType.DMA((4, 8)),
            pltpu.SemaphoreType.DMA((4,)),
            pltpu.SemaphoreType.DMA((2, 6)),
            pltpu.SemaphoreType.DMA((2, 6)),
        ],
        compiler_params=pltpu.CompilerParams(
            collective_id=1, has_side_effects=True, vmem_limit_bytes=32 * 1024 * 1024
        ),
        name="scatter",
    )(o, dq, dk, dv)


def per_device(queries, key_rows, value_rows, out_cotangent, scale_starts):
    q, k, v, g = gather(queries, key_rows, value_rows, out_cotangent)
    o, dq, dk, dv = attention(scale_starts, q, k, v, g)
    return scatter(o, dq, dk, dv)


def solution(mesh):
    rows = P(("dp", "seq"), None)
    return jax.shard_map(
        per_device,
        mesh=mesh,
        in_specs=(rows, rows, rows, rows, P("dp")),
        out_specs=(rows,) * 4,
        check_vma=False,
    )
```

```python
import math

import jax
import jax.numpy as jnp
from jax import lax
from jax.experimental import pallas as pl
from jax.experimental.pallas import tpu as pltpu
from jax.sharding import PartitionSpec as P

HEADS = 8
D = 128
TOK = 128
NX = 4
NZ = 4
COL = NZ * 2 * TOK
HALF = COL // 2
SCALES = 12
QB = 512
FACTOR = 1.0 / math.sqrt(D)
EXP2_FACTOR = FACTOR * math.log2(math.e)
NEG = -1e30
BIG = 1 << 30
MESH = pl.DeviceIdType.MESH
F32 = jnp.float32
BF16 = jnp.bfloat16
PARTNERS = (4, 5, 2, 3, 6, 7, 1)
K, V, Q, G = range(4)
O, DQ, DK, DV = range(4, 8)


def dot(a, b):
    return jnp.dot(a, b, preferred_element_type=F32)


def wide(a):
    return a.astype(F32)


def fused_kernel(
    starts, q_ref, k_ref, v_ref, g_ref, oo, dqo, dko, dvo,
    qg, gg, kg, vg, qt, gt, kt, vt, pt, ot, ms, ls, gs, shr, ins, dqt, sbuf,
    part, land, mid, red, ob, dqb, zs, zr, loc, xs, xr, ys, yr,
):
    s = lax.axis_index("seq")
    x, z, c = s // 8, (s // 2) % 4, s % 2
    me = z * 2 + c

    def device(x, z, c):
        return (lax.axis_index("dp"), lax.rem(x, NX) * 8 + lax.rem(z, NZ) * 2 + lax.rem(c, 2))

    sem = pltpu.get_barrier_semaphore()
    for i in PARTNERS:
        pl.semaphore_signal(sem, inc=1, device_id=device(x, z + i // 2, c + i % 2), device_id_type=MESH)
    for dx in (1, 3):
        pl.semaphore_signal(sem, inc=1, device_id=device(x + dx, z, c), device_id_type=MESH)
    pl.semaphore_wait(sem, len(PARTNERS) + 2)

    def z_copy(a, i):
        pz, pc = lax.rem(z + i // 2, NZ), lax.rem(c + i % 2, 2)
        his = pz * 2 + pc
        if a < 4:
            src = (k_ref, v_ref, q_ref, g_ref)[a].at[:, pl.ds(pl.multiple_of(his * D, D), D)]
            dst = (kg.at[0], vg.at[0], qg, gg)[a].at[pl.ds(pl.multiple_of(me * TOK, TOK), TOK)]
        else:
            src = (ob, dqb, red.at[0], red.at[1])[a - 4].at[pl.ds(pl.multiple_of(his * TOK, TOK), TOK)]
            dst = (oo, dqo, dko, dvo)[a - 4].at[:, pl.ds(pl.multiple_of(me * D, D), D)]
        if i == 0:
            return pltpu.make_async_copy(src, dst, loc.at[a])
        return pltpu.make_async_remote_copy(
            src_ref=src, dst_ref=dst, send_sem=zs.at[a, i], recv_sem=zr.at[a, i],
            device_id=device(x, pz, pc), device_id_type=MESH,
        )

    def z_start(a):
        copies = [z_copy(a, i) for i in (0,) + PARTNERS]
        for copy in copies:
            copy.start()
        return copies

    def z_arrive(copies):
        copies[0].wait()
        for copy in copies[1:]:
            copy.wait_recv()

    def x_copy(sems, a, kind, dx, src, dst):
        copy = pltpu.make_async_remote_copy(
            src_ref=src, dst_ref=dst, send_sem=sems[0].at[a, kind], recv_sem=sems[1].at[a, kind],
            device_id=device(x + dx, z, c), device_id_type=MESH,
        )
        copy.start()
        return copy

    def spread(a, kind, dx, slot, half):
        ref = (kg, vg)[a]
        rows = pl.ds(half * HALF, HALF)
        return x_copy((xs, xr), a, kind, dx, ref.at[slot, rows], ref.at[(slot - dx) % NX, rows])

    zc = [z_start(a) for a in (K, V, Q, G)]

    sub = lax.broadcasted_iota(jnp.int32, (D, COL), 0)
    pos = x * COL + lax.broadcasted_iota(jnp.int32, (D, COL), 1)
    nxt = jnp.full((D, COL), BIG, jnp.int32)
    now = jnp.full((D, COL), BIG, jnp.int32)
    lane = lax.broadcasted_iota(jnp.int32, (1, D), 1)
    starts_row = jnp.full((1, D), BIG, jnp.int32)
    for n in range(SCALES):
        nxt = jnp.where(sub == n, starts[n], nxt)
        now = jnp.where(sub == n + 1, starts[n], now)
        starts_row = jnp.where(lane == n, starts[n], starts_row)
    qt[D:, :] = jnp.where((nxt > pos) & (now <= pos), NEG, 0.0).astype(BF16)

    xc = [None, None]
    for a in (K, V):
        z_arrive(zc[a])
        xc[a] = [spread(a, 0, 1, 0, 0), spread(a, 1, 3, 0, 1), spread(a, 2, 1, 0, 1), spread(a, 3, 3, 0, 0)]

    def forward(a):
        xc[a][0].wait_recv()
        xc[a].append(spread(a, 4, 1, 3, 0))
        xc[a][1].wait_recv()
        xc[a].append(spread(a, 5, 3, 1, 1))

    def transposed(a, slot):
        (kt, vt)[a][slot] = (kg, vg)[a][slot].T

    transposed(K, 0)
    transposed(V, 0)
    forward(K)
    xc[K][2].wait_recv()
    xc[K][3].wait_recv()
    transposed(K, 1)
    transposed(K, 3)
    z_arrive(zc[Q])
    qt[:D, :] = qg[...].T
    xc[K][4].wait_recv()
    xc[K][5].wait_recv()
    transposed(K, 2)

    def scores(n):
        slot, cols = n // 2, pl.ds(n % 2 * QB, QB)
        key_pos = lax.rem(x + slot, NX) * COL + lax.broadcasted_iota(jnp.int32, (COL, D), 0)
        reached = jnp.where(key_pos >= starts_row, 1.0, 0.0).astype(BF16)
        sbuf[n % 2] = dot(jnp.concatenate([kg[slot], reached], axis=1), qt[:, cols])

    def soften(n):
        slot, cols = n // 2, pl.ds(n % 2 * QB, QB)
        scored = sbuf[n % 2]
        m = jnp.max(scored, axis=0, keepdims=True) * EXP2_FACTOR
        p = jnp.exp2(scored * EXP2_FACTOR - m)
        ms[slot, :, cols] = m
        ls[slot, :, cols] = jnp.sum(p, axis=0, keepdims=True)
        half = p.astype(BF16)
        pt[slot, :, cols] = half
        ot[slot, :, cols] = dot(vt[slot], half)

    order = (0, 1, 6, 7, 2, 3, 4, 5)

    def first(begin, end):
        for n in range(begin, end):
            if n + 1 < len(order):
                scores(order[n + 1])
            soften(order[n])

    scores(order[0])
    first(0, 2)
    forward(V)
    xc[V][2].wait_recv()
    xc[V][3].wait_recv()
    transposed(V, 1)
    transposed(V, 3)
    first(2, 6)
    xc[V][4].wait_recv()
    xc[V][5].wait_recv()
    transposed(V, 2)
    first(6, 8)

    z_arrive(zc[G])
    gt[...] = gg[...].T
    top = jnp.maximum(jnp.maximum(ms[0], ms[1]), jnp.maximum(ms[2], ms[3]))
    shares = [jnp.exp2(ms[j] - top) for j in range(NX)]
    inverse = 1.0 / (shares[0] * ls[0] + shares[1] * ls[1] + shares[2] * ls[2] + shares[3] * ls[3])
    shares = [share * inverse for share in shares]
    o = ot[0] * shares[0] + ot[1] * shares[1] + ot[2] * shares[2] + ot[3] * shares[3]
    ob[...] = o.T.astype(BF16)
    zc.append(z_start(O))
    g = wide(gt[...])
    ins[...] = jnp.sum(o * g, axis=0, keepdims=True)
    for j in range(NX):
        gs[j] = (g * shares[j]).T.astype(BF16)
        shr[j] = shares[j]

    def second(slot):
        p = pt[slot]
        ds = (wide(p) * shr[slot] * (dot(vg[slot], gt[...]) - ins[...])).astype(BF16)
        part[0, slot] = (dot(ds, qg[...]) * FACTOR).astype(BF16)
        part[1, slot] = dot(p, gs[slot]).astype(BF16)
        more = dot(kt[slot], ds)
        dqt[...] = more if slot == 2 else dqt[...] + more

    def collect(a, kind, dx, src):
        return x_copy((ys, yr), a, kind, dx, src, land.at[a, kind])

    low, high = pl.ds(0, HALF), pl.ds(HALF, HALF)
    yc = [[None] * 6, [None] * 6]
    second(2)
    for a in range(2):
        yc[a][0] = collect(a, 0, 1, part.at[a, 2, low])
        yc[a][1] = collect(a, 1, 3, part.at[a, 2, high])
    second(1)
    for a in range(2):
        yc[a][2] = collect(a, 2, 1, part.at[a, 1, high])
    second(3)
    for a in range(2):
        yc[a][3] = collect(a, 3, 3, part.at[a, 3, low])
    second(0)
    dqb[...] = (dqt[...] * FACTOR).T.astype(BF16)
    zc.append(z_start(DQ))
    for a in range(2):
        yc[a][0].wait_recv()
        mid[a, 0] = (wide(land[a, 0]) + wide(part[a, 1, low])).astype(BF16)
        yc[a][4] = collect(a, 4, 1, mid.at[a, 0])
        yc[a][1].wait_recv()
        mid[a, 1] = (wide(land[a, 1]) + wide(part[a, 3, high])).astype(BF16)
        yc[a][5] = collect(a, 5, 3, mid.at[a, 1])
    for a in range(2):
        for copy in yc[a][2:]:
            copy.wait_recv()
        red[a, low] = (wide(part[a, 0, low]) + wide(land[a, 4]) + wide(land[a, 3])).astype(BF16)
        red[a, high] = (wide(part[a, 0, high]) + wide(land[a, 5]) + wide(land[a, 2])).astype(BF16)
        zc.append(z_start(DK + a))
    for copies in xc + yc:
        for copy in copies:
            copy.wait_send()
    for a in range(8):
        if a >= 4:
            z_arrive(zc[a])
        for copy in zc[a][1:]:
            copy.wait_send()


def fused(starts, q, k, v, g):
    out = jax.ShapeDtypeStruct((TOK, HEADS * D), BF16)
    anyspace = pl.BlockSpec(memory_space=pl.ANY)
    dma = pltpu.SemaphoreType.DMA
    return pl.pallas_call(
        fused_kernel,
        out_shape=(out,) * 4,
        in_specs=[pl.BlockSpec(memory_space=pltpu.SMEM)] + [anyspace] * 4,
        out_specs=[anyspace] * 4,
        scratch_shapes=[
            pltpu.VMEM((COL, D), BF16),
            pltpu.VMEM((COL, D), BF16),
            pltpu.VMEM((NX, COL, D), BF16),
            pltpu.VMEM((NX, COL, D), BF16),
            pltpu.VMEM((2 * D, COL), BF16),
            pltpu.VMEM((D, COL), BF16),
            pltpu.VMEM((NX, D, COL), BF16),
            pltpu.VMEM((NX, D, COL), BF16),
            pltpu.VMEM((NX, COL, COL), BF16),
            pltpu.VMEM((NX, D, COL), F32),
            pltpu.VMEM((NX, 1, COL), F32),
            pltpu.VMEM((NX, 1, COL), F32),
            pltpu.VMEM((NX, COL, D), BF16),
            pltpu.VMEM((NX, 1, COL), F32),
            pltpu.VMEM((1, COL), F32),
            pltpu.VMEM((D, COL), F32),
            pltpu.VMEM((2, COL, QB), F32),
            pltpu.VMEM((2, NX, COL, D), BF16),
            pltpu.VMEM((2, 6, HALF, D), BF16),
            pltpu.VMEM((2, 2, HALF, D), BF16),
            pltpu.VMEM((2, COL, D), BF16),
            pltpu.VMEM((COL, D), BF16),
            pltpu.VMEM((COL, D), BF16),
            dma((8, 8)),
            dma((8, 8)),
            dma((8,)),
            dma((2, 6)),
            dma((2, 6)),
            dma((2, 6)),
            dma((2, 6)),
        ],
        compiler_params=pltpu.CompilerParams(
            collective_id=0, has_side_effects=True, vmem_limit_bytes=58 * 1024 * 1024
        ),
        name="fused",
    )(starts, q, k, v, g)


def per_device(queries, key_rows, value_rows, out_cotangent, scale_starts):
    return fused(scale_starts, queries, key_rows, value_rows, out_cotangent)


def solution(mesh):
    rows = P(("dp", "seq"), None)
    return jax.shard_map(
        per_device,
        mesh=mesh,
        in_specs=(rows, rows, rows, rows, P("dp")),
        out_specs=(rows,) * 4,
        check_vma=False,
    )
```

```python
import math

import jax
import jax.numpy as jnp
from jax import lax
from jax.experimental import pallas as pl
from jax.experimental.pallas import tpu as pltpu
from jax.sharding import PartitionSpec as P

HEADS = 8
D = 128
TOK = 128
NX = 4
NZ = 4
COL = NZ * 2 * TOK
SCALES = 12
QB = 512
FACTOR = 1.0 / math.sqrt(D)
EXP2_FACTOR = FACTOR * math.log2(math.e)
NEG = -1e30
BIG = 1 << 30
MESH = pl.DeviceIdType.MESH
F32 = jnp.float32
BF16 = jnp.bfloat16
PIECES = (4, 5, 2, 3, 6, 7, 1, 0)
NEAR, FAR = (2, 3, 6, 7, 1, 0), (4, 5)
HALF = COL // 2
K, V, Q, G = range(4)
O, DQ, DV, DK = range(4, 8)


def dot(a, b):
    return jnp.dot(a, b, preferred_element_type=F32)


def wide(a):
    return a.astype(F32)


def fused_kernel(
    starts, q_ref, k_ref, v_ref, g_ref, oo, dqo, dvo, dko,
    qg, gg, kg, vg, qt, gt, kt, vt, pt, ot, ms, ls, gs, shr, ins, dqt, sbuf,
    part, land, mid, red, ob, dqb, zs, zr, xs, xr, ys, yr,
):
    s = lax.axis_index("seq")
    x, z, c = s // 8, (s // 2) % 4, s % 2
    p = x // 2
    guest = (c + p) % 2
    col = x + guest * (3 - 2 * x)
    head = 2 * z + p
    me = c * NZ + z

    def device(x, z, c):
        return (lax.axis_index("dp"), x * 8 + lax.rem(z, NZ) * 2 + lax.rem(c, 2))

    next_x = x + 1 - 2 * (x % 2)
    x_mate, d_mate = device(next_x, z, c), device(x, z, c + 1)
    sem = pltpu.get_barrier_semaphore()
    greeted = [device(x, z + i // 2, c + i % 2) for i in range(1, 8)]
    greeted += [device(3 - x, z + i // 2, c + i % 2) for i in range(8)] + [x_mate]
    for other in greeted:
        pl.semaphore_signal(sem, inc=1, device_id=other, device_id_type=MESH)
    pl.semaphore_wait(sem, len(greeted))

    def z_copy(a, i, local=False):
        far, one = lax.rem(z + i // 2, NZ), i % 2
        if a < 4:
            at = (far * 2 + (p + one) % 2) * D
            src = (k_ref, v_ref, q_ref, g_ref)[a].at[:, pl.ds(pl.multiple_of(at, D), D)]
            dst = (kg.at[0], vg.at[0], qg, gg)[a].at[pl.ds(pl.multiple_of(me * TOK, TOK), TOK)]
            there, kind = device(x + one * (3 - 2 * x), far, p), i // 2 * 2 + c
        else:
            at = (one * NZ + far) * TOK
            src = (ob, dqb, red.at[0], red.at[1])[a - 4].at[pl.ds(pl.multiple_of(at, TOK), TOK)]
            dst = (oo, dqo, dvo, dko)[a - 4].at[:, pl.ds(pl.multiple_of(head * D, D), D)]
            there, kind = device(col, far, one), i // 2 * 2 + guest
        if local:
            return pltpu.make_async_copy(src, dst, zr.at[a, kind])
        return pltpu.make_async_remote_copy(
            src_ref=src, dst_ref=dst, send_sem=zs.at[a, i], recv_sem=zr.at[a, kind],
            device_id=there, device_id_type=MESH,
        )

    def mine(a, i):
        if i > 1 or (i > 0 and a < 4):
            return None
        return (1 - guest) * (1 if a < 4 else 1 - (c + i) % 2) == 1

    def z_start(a, pieces=PIECES):
        for i in pieces:
            own = mine(a, i)
            if own is None:
                z_copy(a, i).start()
            else:
                pl.when(own)(lambda: z_copy(a, i, local=True).start())
                pl.when(jnp.logical_not(own))(lambda: z_copy(a, i).start())

    def z_arrive(a, pieces=PIECES):
        for i in pieces:
            if a < 4:
                dst = (kg.at[0], vg.at[0], qg, gg)[a].at[pl.ds(0, TOK)]
            else:
                dst = (oo, dqo, dvo, dko)[a - 4].at[:, pl.ds(0, D)]
            pltpu.make_async_copy(dst, dst, zr.at[a, i]).wait()

    def z_sent(a):
        for i in PIECES:
            own = mine(a, i)
            if own is None:
                z_copy(a, i).wait_send()
            else:
                pl.when(jnp.logical_not(own))(lambda: z_copy(a, i).wait_send())

    def to(mate, sems, a, kind, src, dst):
        copy = pltpu.make_async_remote_copy(
            src_ref=src, dst_ref=dst, send_sem=sems[0].at[a, kind], recv_sem=sems[1].at[a, kind],
            device_id=mate, device_id_type=MESH,
        )
        copy.start()
        return copy

    places = (col, col + 1 - 2 * (col % 2), 3 - col, 2 - col + 2 * (col % 2))

    def position(rows):
        return (rows >> 7 & 3) * 256 + (rows >> 9) * 128 + (rows & 127)

    z_start(K)
    z_start(V)

    sub = lax.broadcasted_iota(jnp.int32, (D, COL), 0)
    pos = col * COL + position(lax.broadcasted_iota(jnp.int32, (D, COL), 1))
    nxt = jnp.full((D, COL), BIG, jnp.int32)
    now = jnp.full((D, COL), BIG, jnp.int32)
    lane = lax.broadcasted_iota(jnp.int32, (1, D), 1)
    starts_row = jnp.full((1, D), BIG, jnp.int32)
    for n in range(SCALES):
        nxt = jnp.where(sub == n, starts[n], nxt)
        now = jnp.where(sub == n + 1, starts[n], now)
        starts_row = jnp.where(lane == n, starts[n], starts_row)
    qt[D:, :] = jnp.where((nxt > pos) & (now <= pos), NEG, 0.0).astype(BF16)

    xc = [None, None]

    def spread(a):
        z_arrive(a)
        ref = (kg, vg)[a]
        xc[a] = [to(x_mate, (xs, xr), a, 0, ref.at[0], ref.at[1]), to(d_mate, (xs, xr), a, 1, ref.at[0], ref.at[2])]

    def forward(a):
        ref = (kg, vg)[a]
        xc[a][0].wait_recv()
        xc[a].append(to(d_mate, (xs, xr), a, 2, ref.at[1], ref.at[3]))

    def transposed(a, slot):
        (kt, vt)[a][slot] = (kg, vg)[a][slot].T

    spread(K)
    z_start(Q)
    transposed(K, 0)
    spread(V)
    transposed(V, 0)
    xc[K][1].wait_recv()
    transposed(K, 2)
    forward(K)
    transposed(K, 1)
    xc[V][1].wait_recv()
    transposed(V, 2)
    z_arrive(Q, NEAR)
    z_start(G)
    z_arrive(Q, FAR)
    qt[:D, :] = qg[...].T
    xc[K][2].wait_recv()
    transposed(K, 3)

    def scores(n):
        slot, cols = n // 2, pl.ds(n % 2 * QB, QB)
        key_pos = places[slot] * COL + position(lax.broadcasted_iota(jnp.int32, (COL, D), 0))
        reached = jnp.where(key_pos >= starts_row, 1.0, 0.0).astype(BF16)
        sbuf[n % 2] = dot(jnp.concatenate([kg[slot], reached], axis=1), qt[:, cols])

    def soften(n):
        slot, cols = n // 2, pl.ds(n % 2 * QB, QB)
        scored = sbuf[n % 2]
        m = jnp.max(scored, axis=0, keepdims=True) * EXP2_FACTOR
        p = jnp.exp2(scored * EXP2_FACTOR - m)
        ms[slot, :, cols] = m
        ls[slot, :, cols] = jnp.sum(p, axis=0, keepdims=True)
        half = p.astype(BF16)
        pt[slot, :, cols] = half
        ot[slot, :, cols] = dot(vt[slot], half)

    order = (0, 1, 4, 5, 2, 3, 6, 7)

    def first(begin, end):
        for n in range(begin, end):
            if n + 1 < len(order):
                scores(order[n + 1])
            soften(order[n])

    scores(order[0])
    first(0, 3)
    forward(V)
    transposed(V, 1)
    first(3, 6)
    xc[V][2].wait_recv()
    transposed(V, 3)
    first(6, 8)

    top = jnp.maximum(jnp.maximum(ms[0], ms[1]), jnp.maximum(ms[2], ms[3]))
    shares = [jnp.exp2(ms[j] - top) for j in range(NX)]
    inverse = 1.0 / (shares[0] * ls[0] + shares[1] * ls[1] + shares[2] * ls[2] + shares[3] * ls[3])
    shares = [share * inverse for share in shares]
    o = ot[0] * shares[0] + ot[1] * shares[1] + ot[2] * shares[2] + ot[3] * shares[3]
    ot[0] = o
    ob[...] = o.astype(BF16).T
    z_start(O)
    for j in range(NX):
        shr[j] = shares[j]
    z_arrive(G)
    gt[...] = gg[...].T

    def scaled(slot):
        gs[slot] = (wide(gt[...]) * shr[slot]).astype(BF16).T

    def second(slot):
        ds = (wide(pt[slot]) * shr[slot] * (dot(vg[slot], gt[...]) - ins[...])).astype(BF16)
        part[1, slot] = (dot(ds, qg[...]) * FACTOR).astype(BF16)
        more = dot(kt[slot], ds)
        dqt[...] = more if slot == 3 else dqt[...] + more

    yc = [[None] * 4, [None] * 4]

    def to_core(a, kind, slot):
        yc[a][kind] = to(d_mate, (ys, yr), a, kind, part.at[a, slot], land.at[a, kind])

    def to_chip(a):
        yc[a][0].wait_recv()
        for half in range(2):
            rows = pl.ds(half * HALF, HALF)
            mid[a, rows] = (wide(part[a, 1, rows]) + wide(land[a, 0, rows])).astype(BF16)
            yc[a][2 + half] = to(x_mate, (ys, yr), a, 2 + half, mid.at[a, rows], land.at[a, 2, rows])

    def total(a):
        for half in range(2):
            rows = pl.ds(half * HALF, HALF)
            if half == 0:
                yc[a][1].wait_recv()
            yc[a][2 + half].wait_recv()
            red[a, rows] = (wide(part[a, 0, rows]) + wide(land[a, 1, rows]) + wide(land[a, 2, rows])).astype(BF16)
            z_start(DV + a, [i for i in PIECES if i % 2 == half])

    def value_part(slot):
        scaled(slot)
        part[0, slot] = dot(pt[slot], gs[slot]).astype(BF16)

    value_part(3)
    to_core(0, 0, 3)
    value_part(1)
    to_chip(0)
    value_part(2)
    to_core(0, 1, 2)
    value_part(0)
    ins[...] = jnp.sum(ot[0] * wide(gt[...]), axis=0, keepdims=True)
    second(3)
    to_core(1, 0, 3)
    second(1)
    to_chip(1)
    total(0)
    second(2)
    to_core(1, 1, 2)
    second(0)
    dqb[...] = (dqt[...] * FACTOR).astype(BF16).T
    z_start(DQ)
    total(1)
    for copies in xc + yc:
        for copy in copies:
            copy.wait_send()
    for a in range(4, 8):
        z_arrive(a)
    for a in range(8):
        z_sent(a)


def fused(starts, q, k, v, g):
    out = jax.ShapeDtypeStruct((TOK, HEADS * D), BF16)
    anyspace = pl.BlockSpec(memory_space=pl.ANY)
    dma = pltpu.SemaphoreType.DMA
    return pl.pallas_call(
        fused_kernel,
        out_shape=(out,) * 4,
        in_specs=[pl.BlockSpec(memory_space=pltpu.SMEM)] + [anyspace] * 4,
        out_specs=[anyspace] * 4,
        scratch_shapes=[
            pltpu.VMEM((COL, D), BF16),
            pltpu.VMEM((COL, D), BF16),
            pltpu.VMEM((NX, COL, D), BF16),
            pltpu.VMEM((NX, COL, D), BF16),
            pltpu.VMEM((2 * D, COL), BF16),
            pltpu.VMEM((D, COL), BF16),
            pltpu.VMEM((NX, D, COL), BF16),
            pltpu.VMEM((NX, D, COL), BF16),
            pltpu.VMEM((NX, COL, COL), BF16),
            pltpu.VMEM((NX, D, COL), F32),
            pltpu.VMEM((NX, 1, COL), F32),
            pltpu.VMEM((NX, 1, COL), F32),
            pltpu.VMEM((NX, COL, D), BF16),
            pltpu.VMEM((NX, 1, COL), F32),
            pltpu.VMEM((1, COL), F32),
            pltpu.VMEM((D, COL), F32),
            pltpu.VMEM((2, COL, QB), F32),
            pltpu.VMEM((2, NX, COL, D), BF16),
            pltpu.VMEM((2, 3, COL, D), BF16),
            pltpu.VMEM((2, COL, D), BF16),
            pltpu.VMEM((2, COL, D), BF16),
            pltpu.VMEM((COL, D), BF16),
            pltpu.VMEM((COL, D), BF16),
            dma((8, 8)),
            dma((8, 8)),
            dma((2, 3)),
            dma((2, 3)),
            dma((2, 4)),
            dma((2, 4)),
        ],
        compiler_params=pltpu.CompilerParams(
            collective_id=0, has_side_effects=True, vmem_limit_bytes=58 * 1024 * 1024
        ),
        name="fused",
    )(starts, q, k, v, g)


def handed_on_kernel(*refs):
    for n in range(4):
        refs[4 + n][...] = refs[n][...]


def handed_on(*arrays):
    vm = pl.BlockSpec(memory_space=pltpu.VMEM)
    return pl.pallas_call(
        handed_on_kernel,
        out_shape=tuple(jax.ShapeDtypeStruct(a.shape, a.dtype) for a in arrays),
        in_specs=[vm] * 4,
        out_specs=[vm] * 4,
        name="handed_on",
    )(*arrays)


def per_device(queries, key_rows, value_rows, out_cotangent, scale_starts):
    attended, query_grad, value_grad, key_grad = fused(scale_starts, queries, key_rows, value_rows, out_cotangent)
    return handed_on(attended, query_grad, key_grad, value_grad)


def solution(mesh):
    rows = P(("dp", "seq"), None)
    return jax.shard_map(
        per_device,
        mesh=mesh,
        in_specs=(rows, rows, rows, rows, P("dp")),
        out_specs=(rows,) * 4,
        check_vma=False,
    )
```

```python
import math

import jax
import jax.numpy as jnp
from jax import lax
from jax.experimental import pallas as pl
from jax.experimental.pallas import tpu as pltpu
from jax.sharding import PartitionSpec as P

HEADS = 8
D = 128
TOK = 128
NX = 4
NZ = 4
COL = NZ * 2 * TOK
SCALES = 12
QB = 512
FACTOR = 1.0 / math.sqrt(D)
EXP2_FACTOR = FACTOR * math.log2(math.e)
NEG = -1e30
BIG = 1 << 30
MESH = pl.DeviceIdType.MESH
F32 = jnp.float32
BF16 = jnp.bfloat16
PIECES = (4, 5, 2, 3, 6, 7, 1, 0)
INWARD = (5, 4, 3, 7, 2, 6, 1, 0)
NEAR, FAR = (2, 3, 6, 7, 1, 0), (4, 5)
HALF = COL // 2
K, V, Q, G = range(4)
O, DQ, DV, DK = range(4, 8)


def dot(a, b):
    return jnp.dot(a, b, preferred_element_type=F32)


def wide(a):
    return a.astype(F32)


def fused_kernel(
    starts, q_ref, k_ref, v_ref, g_ref, oo, dqo, dvo, dko,
    qg, gg, kg, vg, qt, gt, kt, vt, pt, ot, ms, ls, gs, shr, ins, dqt, sbuf,
    part, land, mid, red, ob, dqb, zs, zr, xs, xr, ys, yr,
):
    s = lax.axis_index("seq")
    x, z, c = s // 8, (s // 2) % 4, s % 2
    p = x // 2
    guest = (c + p) % 2
    col = x + guest * (3 - 2 * x)
    head = 2 * z + p
    me = c * NZ + z

    def device(x, z, c):
        return (lax.axis_index("dp"), x * 8 + lax.rem(z, NZ) * 2 + lax.rem(c, 2))

    next_x = x + 1 - 2 * (x % 2)
    x_mate, d_mate = device(next_x, z, c), device(x, z, c + 1)
    sem = pltpu.get_barrier_semaphore()
    greeted = [device(x, z + i // 2, c + i % 2) for i in range(1, 8)]
    greeted += [device(3 - x, z + i // 2, c + i % 2) for i in range(8)] + [x_mate]
    for other in greeted:
        pl.semaphore_signal(sem, inc=1, device_id=other, device_id_type=MESH)
    pl.semaphore_wait(sem, len(greeted))

    def z_copy(a, i, local=False):
        far, one = lax.rem(z + i // 2, NZ), i % 2
        if a < 4:
            at = (far * 2 + (p + one) % 2) * D
            src = (k_ref, v_ref, q_ref, g_ref)[a].at[:, pl.ds(pl.multiple_of(at, D), D)]
            dst = (kg.at[0], vg.at[0], qg, gg)[a].at[pl.ds(pl.multiple_of(me * TOK, TOK), TOK)]
            there = device(x + one * (3 - 2 * x), far, p)
        else:
            at = (one * NZ + far) * TOK
            src = (ob, dqb, red.at[0], red.at[1])[a - 4].at[pl.ds(pl.multiple_of(at, TOK), TOK)]
            dst = (oo, dqo, dvo, dko)[a - 4].at[:, pl.ds(pl.multiple_of(head * D, D), D)]
            there = device(col, far, one)
        kind = 0 if i in FAR else 1
        if local:
            return pltpu.make_async_copy(src, dst, zr.at[a, kind])
        return pltpu.make_async_remote_copy(
            src_ref=src, dst_ref=dst, send_sem=zs.at[a, kind], recv_sem=zr.at[a, kind],
            device_id=there, device_id_type=MESH,
        )

    def mine(a, i):
        if i > 1 or (i > 0 and a < 4):
            return None
        return (1 - guest) * (1 if a < 4 else 1 - (c + i) % 2) == 1

    def z_start(a, pieces=PIECES):
        for i in INWARD if a < 4 else pieces:
            own = mine(a, i)
            if own is None:
                z_copy(a, i).start()
            else:
                pl.when(own)(lambda: z_copy(a, i, local=True).start())
                pl.when(jnp.logical_not(own))(lambda: z_copy(a, i).start())

    def pieces_wait(sem, count):
        block = red.at[0, pl.ds(0, count * TOK)]
        pltpu.make_async_copy(block, block, sem).wait()

    def z_arrive(a, pieces=PIECES):
        if FAR[0] in pieces:
            pieces_wait(zr.at[a, 0], len(FAR))
        if NEAR[0] in pieces:
            pieces_wait(zr.at[a, 1], len(NEAR))

    def z_sent(a):
        pieces_wait(zs.at[a, 0], len(FAR))
        pieces_wait(zs.at[a, 1], len(NEAR) - 1)
        pl.when(guest == 1)(lambda: pieces_wait(zs.at[a, 1], 1))

    def to(mate, sems, a, kind, src, dst):
        copy = pltpu.make_async_remote_copy(
            src_ref=src, dst_ref=dst, send_sem=sems[0].at[a, kind], recv_sem=sems[1].at[a, kind],
            device_id=mate, device_id_type=MESH,
        )
        copy.start()
        return copy

    places = (col, col + 1 - 2 * (col % 2), 3 - col, 2 - col + 2 * (col % 2))

    def position(rows):
        return (rows >> 7 & 3) * 256 + (rows >> 9) * 128 + (rows & 127)

    z_start(K)
    z_start(V)

    sub = lax.broadcasted_iota(jnp.int32, (D, COL), 0)
    pos = col * COL + position(lax.broadcasted_iota(jnp.int32, (D, COL), 1))
    nxt = jnp.full((D, COL), BIG, jnp.int32)
    now = jnp.full((D, COL), BIG, jnp.int32)
    lane = lax.broadcasted_iota(jnp.int32, (1, D), 1)
    starts_row = jnp.full((1, D), BIG, jnp.int32)
    for n in range(SCALES):
        nxt = jnp.where(sub == n, starts[n], nxt)
        now = jnp.where(sub == n + 1, starts[n], now)
        starts_row = jnp.where(lane == n, starts[n], starts_row)
    qt[D:, :] = jnp.where((nxt > pos) & (now <= pos), NEG, 0.0).astype(BF16)

    xc = [None, None]

    def spread(a):
        z_arrive(a)
        ref = (kg, vg)[a]
        xc[a] = [to(x_mate, (xs, xr), a, 0, ref.at[0], ref.at[1]), to(d_mate, (xs, xr), a, 1, ref.at[0], ref.at[2])]

    def forward(a):
        ref = (kg, vg)[a]
        xc[a][0].wait_recv()
        xc[a].append(to(d_mate, (xs, xr), a, 2, ref.at[1], ref.at[3]))

    def transposed(a, slot):
        (kt, vt)[a][slot] = (kg, vg)[a][slot].T

    spread(K)
    z_start(Q)
    transposed(K, 0)
    spread(V)
    transposed(V, 0)
    xc[K][1].wait_recv()
    transposed(K, 2)
    forward(K)
    transposed(K, 1)
    xc[V][1].wait_recv()
    transposed(V, 2)
    z_arrive(Q, NEAR)
    z_start(G)
    z_arrive(Q, FAR)
    qt[:D, :] = qg[...].T
    xc[K][2].wait_recv()
    transposed(K, 3)

    def scores(n):
        slot, cols = n // 2, pl.ds(n % 2 * QB, QB)
        key_pos = places[slot] * COL + position(lax.broadcasted_iota(jnp.int32, (COL, D), 0))
        reached = jnp.where(key_pos >= starts_row, 1.0, 0.0).astype(BF16)
        sbuf[n % 2] = dot(jnp.concatenate([kg[slot], reached], axis=1), qt[:, cols])

    def soften(n):
        slot, cols = n // 2, pl.ds(n % 2 * QB, QB)
        scored = sbuf[n % 2]
        m = jnp.max(scored, axis=0, keepdims=True) * EXP2_FACTOR
        p = jnp.exp2(scored * EXP2_FACTOR - m)
        ms[slot, :, cols] = m
        ls[slot, :, cols] = jnp.sum(p, axis=0, keepdims=True)
        half = p.astype(BF16)
        pt[slot, :, cols] = half
        ot[slot, :, cols] = dot(vt[slot], half)

    order = (0, 1, 4, 5, 2, 3, 6, 7)

    def first(begin, end):
        for n in range(begin, end):
            if n + 1 < len(order):
                scores(order[n + 1])
            soften(order[n])

    scores(order[0])
    first(0, 3)
    forward(V)
    transposed(V, 1)
    first(3, 6)
    xc[V][2].wait_recv()
    transposed(V, 3)
    first(6, 8)

    top = jnp.maximum(jnp.maximum(ms[0], ms[1]), jnp.maximum(ms[2], ms[3]))
    shares = [jnp.exp2(ms[j] - top) for j in range(NX)]
    inverse = 1.0 / (shares[0] * ls[0] + shares[1] * ls[1] + shares[2] * ls[2] + shares[3] * ls[3])
    shares = [share * inverse for share in shares]
    o = ot[0] * shares[0] + ot[1] * shares[1] + ot[2] * shares[2] + ot[3] * shares[3]
    ot[0] = o
    ob[...] = o.astype(BF16).T
    z_start(O)
    for j in range(NX):
        shr[j] = shares[j]
    z_arrive(G)
    gt[...] = gg[...].T

    def scaled(slot):
        gs[slot] = (wide(gt[...]) * shr[slot]).astype(BF16).T

    def second(slot):
        ds = (wide(pt[slot]) * shr[slot] * (dot(vg[slot], gt[...]) - ins[...])).astype(BF16)
        part[1, slot] = (dot(ds, qg[...]) * FACTOR).astype(BF16)
        more = dot(kt[slot], ds)
        dqt[...] = more if slot == 3 else dqt[...] + more

    yc = [[None] * 4, [None] * 4]

    def to_core(a, kind, slot):
        yc[a][kind] = to(d_mate, (ys, yr), a, kind, part.at[a, slot], land.at[a, kind])

    def to_chip(a):
        yc[a][0].wait_recv()
        for half in range(2):
            rows = pl.ds(half * HALF, HALF)
            mid[a, rows] = (wide(part[a, 1, rows]) + wide(land[a, 0, rows])).astype(BF16)
            yc[a][2 + half] = to(x_mate, (ys, yr), a, 2 + half, mid.at[a, rows], land.at[a, 2, rows])

    def total(a, halves=(0, 1)):
        for half in halves:
            rows = pl.ds(half * HALF, HALF)
            if half == 0:
                yc[a][1].wait_recv()
            yc[a][2 + half].wait_recv()
            red[a, rows] = (wide(part[a, 0, rows]) + wide(land[a, 1, rows]) + wide(land[a, 2, rows])).astype(BF16)
            z_start(DV + a, [i for i in PIECES if i % 2 == half])

    def value_part(slot):
        scaled(slot)
        part[0, slot] = dot(pt[slot], gs[slot]).astype(BF16)

    value_part(3)
    to_core(0, 0, 3)
    value_part(1)
    to_chip(0)
    value_part(2)
    to_core(0, 1, 2)
    value_part(0)
    ins[...] = jnp.sum(ot[0] * wide(gt[...]), axis=0, keepdims=True)
    second(3)
    to_core(1, 0, 3)
    total(0, (0,))
    second(1)
    to_chip(1)
    total(0, (1,))
    second(2)
    to_core(1, 1, 2)
    second(0)
    dqb[...] = (dqt[...] * FACTOR).astype(BF16).T
    z_start(DQ)
    total(1)
    for copies in xc + yc:
        for copy in copies:
            copy.wait_send()
    for a in range(4, 8):
        z_arrive(a)
    for a in range(8):
        z_sent(a)


def fused(starts, q, k, v, g):
    out = jax.ShapeDtypeStruct((TOK, HEADS * D), BF16)
    anyspace = pl.BlockSpec(memory_space=pl.ANY)
    dma = pltpu.SemaphoreType.DMA
    return pl.pallas_call(
        fused_kernel,
        out_shape=(out,) * 4,
        in_specs=[pl.BlockSpec(memory_space=pltpu.SMEM)] + [anyspace] * 4,
        out_specs=[anyspace] * 4,
        scratch_shapes=[
            pltpu.VMEM((COL, D), BF16),
            pltpu.VMEM((COL, D), BF16),
            pltpu.VMEM((NX, COL, D), BF16),
            pltpu.VMEM((NX, COL, D), BF16),
            pltpu.VMEM((2 * D, COL), BF16),
            pltpu.VMEM((D, COL), BF16),
            pltpu.VMEM((NX, D, COL), BF16),
            pltpu.VMEM((NX, D, COL), BF16),
            pltpu.VMEM((NX, COL, COL), BF16),
            pltpu.VMEM((NX, D, COL), F32),
            pltpu.VMEM((NX, 1, COL), F32),
            pltpu.VMEM((NX, 1, COL), F32),
            pltpu.VMEM((NX, COL, D), BF16),
            pltpu.VMEM((NX, 1, COL), F32),
            pltpu.VMEM((1, COL), F32),
            pltpu.VMEM((D, COL), F32),
            pltpu.VMEM((2, COL, QB), F32),
            pltpu.VMEM((2, NX, COL, D), BF16),
            pltpu.VMEM((2, 3, COL, D), BF16),
            pltpu.VMEM((2, COL, D), BF16),
            pltpu.VMEM((2, COL, D), BF16),
            pltpu.VMEM((COL, D), BF16),
            pltpu.VMEM((COL, D), BF16),
            dma((8, 2)),
            dma((8, 2)),
            dma((2, 3)),
            dma((2, 3)),
            dma((2, 4)),
            dma((2, 4)),
        ],
        compiler_params=pltpu.CompilerParams(
            collective_id=0, has_side_effects=True, vmem_limit_bytes=58 * 1024 * 1024
        ),
        name="fused",
    )(starts, q, k, v, g)


def handed_on_kernel(*refs):
    given, taken, (held, come, gone) = refs[:4], refs[4:8], refs[8:]
    into = [pltpu.make_async_copy(given[n], held.at[n], come.at[n]) for n in range(4)]
    out = [pltpu.make_async_copy(held.at[n], taken[n], gone.at[n]) for n in range(4)]
    for copy in into:
        copy.start()
    for n in range(4):
        into[n].wait()
        out[n].start()
    for copy in out:
        copy.wait()


def handed_on(*arrays):
    anyspace = pl.BlockSpec(memory_space=pl.ANY)
    return pl.pallas_call(
        handed_on_kernel,
        out_shape=tuple(jax.ShapeDtypeStruct(a.shape, a.dtype) for a in arrays),
        in_specs=[anyspace] * 4,
        out_specs=[anyspace] * 4,
        scratch_shapes=[
            pltpu.VMEM((4,) + arrays[0].shape, arrays[0].dtype),
            pltpu.SemaphoreType.DMA((4,)),
            pltpu.SemaphoreType.DMA((4,)),
        ],
        compiler_params=pltpu.CompilerParams(vmem_limit_bytes=58 * 1024 * 1024),
        name="handed_on",
    )(*arrays)


def per_device(queries, key_rows, value_rows, out_cotangent, scale_starts):
    attended, query_grad, value_grad, key_grad = fused(scale_starts, queries, key_rows, value_rows, out_cotangent)
    return handed_on(attended, query_grad, key_grad, value_grad)


def solution(mesh):
    rows = P(("dp", "seq"), None)
    return jax.shard_map(
        per_device,
        mesh=mesh,
        in_specs=(rows, rows, rows, rows, P("dp")),
        out_specs=(rows,) * 4,
        check_vma=False,
    )
```

```python
import math

import jax
import jax.numpy as jnp
from jax import lax
from jax.experimental import pallas as pl
from jax.experimental.pallas import tpu as pltpu
from jax.sharding import PartitionSpec as P

HEADS = 8
D = 128
TOK = 128
NX = 4
NZ = 4
COL = NZ * 2 * TOK
SCALES = 12
QB = 512
FACTOR = 1.0 / math.sqrt(D)
EXP2_FACTOR = FACTOR * math.log2(math.e)
NEG = -1e30
BIG = 1 << 30
MESH = pl.DeviceIdType.MESH
F32 = jnp.float32
BF16 = jnp.bfloat16
PIECES = (4, 5, 2, 3, 6, 7, 1, 0)
INWARD = (5, 4, 3, 7, 2, 6, 1, 0)
NEAR, FAR = (2, 3, 6, 7, 1, 0), (4, 5)
HALF = COL // 2
K, V, Q, G = range(4)
O, DQ, DV, DK = range(4, 8)


def dot(a, b):
    return jnp.dot(a, b, preferred_element_type=F32)


def wide(a):
    return a.astype(F32)


def fused_kernel(
    starts, q_ref, k_ref, v_ref, g_ref, oo, dqo, dvo, dko,
    qg, gg, kg, vg, qt, gt, kt, vt, pt, ot, ms, ls, gs, shr, ins, dqt, sbuf,
    part, land, mid, red, ob, dqb, zs, zr, xs, xr, ys, yr,
):
    s = lax.axis_index("seq")
    x, z, c = s // 8, (s // 2) % 4, s % 2
    p = x // 2
    guest = (c + p) % 2
    col = x + guest * (3 - 2 * x)
    head = 2 * z + p
    me = c * NZ + z

    def device(x, z, c):
        return (lax.axis_index("dp"), x * 8 + lax.rem(z, NZ) * 2 + lax.rem(c, 2))

    next_x = x + 1 - 2 * (x % 2)
    x_mate, d_mate = device(next_x, z, c), device(x, z, c + 1)
    sem = pltpu.get_barrier_semaphore()
    greeted = [device(x, z + i // 2, c + i % 2) for i in range(1, 8)]
    greeted += [device(3 - x, z + i // 2, c + i % 2) for i in range(8)] + [x_mate]
    for other in greeted:
        pl.semaphore_signal(sem, inc=1, device_id=other, device_id_type=MESH)
    pl.semaphore_wait(sem, len(greeted))

    def z_copy(a, i, local=False):
        far, one = lax.rem(z + i // 2, NZ), i % 2
        if a < 4:
            at = (far * 2 + (p + one) % 2) * D
            src = (k_ref, v_ref, q_ref, g_ref)[a].at[:, pl.ds(pl.multiple_of(at, D), D)]
            dst = (kg.at[0], vg.at[0], qg, gg)[a].at[pl.ds(pl.multiple_of(me * TOK, TOK), TOK)]
            there = device(x + one * (3 - 2 * x), far, p)
        else:
            at = (one * NZ + far) * TOK
            src = (ob, dqb, red.at[0], red.at[1])[a - 4].at[pl.ds(pl.multiple_of(at, TOK), TOK)]
            dst = (oo, dqo, dvo, dko)[a - 4].at[:, pl.ds(pl.multiple_of(head * D, D), D)]
            there = device(col, far, one)
        kind = 0 if i in FAR else 1
        if local:
            return pltpu.make_async_copy(src, dst, zr.at[a, kind])
        return pltpu.make_async_remote_copy(
            src_ref=src, dst_ref=dst, send_sem=zs.at[a, kind], recv_sem=zr.at[a, kind],
            device_id=there, device_id_type=MESH,
        )

    def mine(a, i):
        if i > 1 or (i > 0 and a < 4):
            return None
        return (1 - guest) * (1 if a < 4 else 1 - (c + i) % 2) == 1

    def z_start(a, pieces=PIECES):
        for i in INWARD if a < 4 else pieces:
            own = mine(a, i)
            if own is None:
                z_copy(a, i).start()
            else:
                pl.when(own)(lambda: z_copy(a, i, local=True).start())
                pl.when(jnp.logical_not(own))(lambda: z_copy(a, i).start())

    def pieces_wait(sem, count):
        block = red.at[0, pl.ds(0, count * TOK)]
        pltpu.make_async_copy(block, block, sem).wait()

    def z_arrive(a, pieces=PIECES):
        if FAR[0] in pieces:
            pieces_wait(zr.at[a, 0], len(FAR))
        if NEAR[0] in pieces:
            pieces_wait(zr.at[a, 1], len(NEAR))

    def z_sent(a):
        pieces_wait(zs.at[a, 0], len(FAR))
        pieces_wait(zs.at[a, 1], len(NEAR) - 1)
        pl.when(guest == 1)(lambda: pieces_wait(zs.at[a, 1], 1))

    def to(mate, sems, a, kind, src, dst):
        copy = pltpu.make_async_remote_copy(
            src_ref=src, dst_ref=dst, send_sem=sems[0].at[a, kind], recv_sem=sems[1].at[a, kind],
            device_id=mate, device_id_type=MESH,
        )
        copy.start()
        return copy

    places = (col, col + 1 - 2 * (col % 2), 3 - col, 2 - col + 2 * (col % 2))

    def position(rows):
        return (rows >> 7 & 3) * 256 + (rows >> 9) * 128 + (rows & 127)

    z_start(K)
    z_start(V)

    sub = lax.broadcasted_iota(jnp.int32, (D, COL), 0)
    pos = col * COL + position(lax.broadcasted_iota(jnp.int32, (D, COL), 1))
    nxt = jnp.full((D, COL), BIG, jnp.int32)
    now = jnp.full((D, COL), BIG, jnp.int32)
    lane = lax.broadcasted_iota(jnp.int32, (1, D), 1)
    starts_row = jnp.full((1, D), BIG, jnp.int32)
    for n in range(SCALES):
        nxt = jnp.where(sub == n, starts[n], nxt)
        now = jnp.where(sub == n + 1, starts[n], now)
        starts_row = jnp.where(lane == n, starts[n], starts_row)
    qt[D:, :] = jnp.where((nxt > pos) & (now <= pos), NEG, 0.0).astype(BF16)

    xc = [None, None]

    def spread(a):
        z_arrive(a)
        ref = (kg, vg)[a]
        xc[a] = [to(x_mate, (xs, xr), a, 0, ref.at[0], ref.at[1]), to(d_mate, (xs, xr), a, 1, ref.at[0], ref.at[2])]

    def forward(a):
        ref = (kg, vg)[a]
        xc[a][0].wait_recv()
        xc[a].append(to(d_mate, (xs, xr), a, 2, ref.at[1], ref.at[3]))

    def transposed(a, slot):
        (kt, vt)[a][slot] = (kg, vg)[a][slot].T

    spread(K)
    z_start(Q)
    transposed(K, 0)
    spread(V)
    transposed(V, 0)
    xc[K][1].wait_recv()
    transposed(K, 2)
    forward(K)
    transposed(K, 1)
    xc[V][1].wait_recv()
    transposed(V, 2)
    z_arrive(Q, NEAR)
    z_start(G)
    z_arrive(Q, FAR)
    qt[:D, :] = qg[...].T
    xc[K][2].wait_recv()
    transposed(K, 3)

    def scores(n):
        slot, cols = n // 2, pl.ds(n % 2 * QB, QB)
        key_pos = places[slot] * COL + position(lax.broadcasted_iota(jnp.int32, (COL, D), 0))
        reached = jnp.where(key_pos >= starts_row, 1.0, 0.0).astype(BF16)
        sbuf[n % 2] = dot(jnp.concatenate([kg[slot], reached], axis=1), qt[:, cols])

    def soften(n):
        slot, cols = n // 2, pl.ds(n % 2 * QB, QB)
        scored = sbuf[n % 2]
        m = jnp.max(scored, axis=0, keepdims=True) * EXP2_FACTOR
        p = jnp.exp2(scored * EXP2_FACTOR - m)
        ms[slot, :, cols] = m
        ls[slot, :, cols] = jnp.sum(p, axis=0, keepdims=True)
        half = p.astype(BF16)
        pt[slot, :, cols] = half
        ot[slot, :, cols] = dot(vt[slot], half)

    order = (0, 1, 4, 5, 2, 3, 6, 7)

    def first(begin, end):
        for n in range(begin, end):
            if n + 1 < len(order):
                scores(order[n + 1])
            soften(order[n])

    scores(order[0])
    first(0, 3)
    forward(V)
    transposed(V, 1)
    first(3, 6)
    xc[V][2].wait_recv()
    transposed(V, 3)
    first(6, 8)

    top = jnp.maximum(jnp.maximum(ms[0], ms[1]), jnp.maximum(ms[2], ms[3]))
    shares = [jnp.exp2(ms[j] - top) for j in range(NX)]
    inverse = 1.0 / (shares[0] * ls[0] + shares[1] * ls[1] + shares[2] * ls[2] + shares[3] * ls[3])
    shares = [share * inverse for share in shares]
    o = ot[0] * shares[0] + ot[1] * shares[1] + ot[2] * shares[2] + ot[3] * shares[3]
    ot[0] = o
    ob[...] = o.astype(BF16).T
    z_start(O, FAR)
    for j in range(NX):
        shr[j] = shares[j]
    z_arrive(G)
    gt[...] = gg[...].T

    def scaled(slot):
        gs[slot] = (wide(gt[...]) * shr[slot]).astype(BF16).T

    def second(slot):
        ds = (wide(pt[slot]) * shr[slot] * (dot(vg[slot], gt[...]) - ins[...])).astype(BF16)
        part[1, slot] = (dot(ds, qg[...]) * FACTOR).astype(BF16)
        more = dot(kt[slot], ds)
        dqt[...] = more if slot == 3 else dqt[...] + more

    yc = [[None] * 4, [None] * 4]

    def to_core(a, kind, slot):
        yc[a][kind] = to(d_mate, (ys, yr), a, kind, part.at[a, slot], land.at[a, kind])

    def to_chip(a):
        yc[a][0].wait_recv()
        for half in range(2):
            rows = pl.ds(half * HALF, HALF)
            mid[a, rows] = (wide(part[a, 1, rows]) + wide(land[a, 0, rows])).astype(BF16)
            yc[a][2 + half] = to(x_mate, (ys, yr), a, 2 + half, mid.at[a, rows], land.at[a, 2, rows])

    def total(a, halves=(0, 1)):
        for half in halves:
            rows = pl.ds(half * HALF, HALF)
            if half == 0:
                yc[a][1].wait_recv()
            yc[a][2 + half].wait_recv()
            red[a, rows] = (wide(part[a, 0, rows]) + wide(land[a, 1, rows]) + wide(land[a, 2, rows])).astype(BF16)
            z_start(DV + a, [i for i in PIECES if i % 2 == half])

    def value_part(slot):
        scaled(slot)
        part[0, slot] = dot(pt[slot], gs[slot]).astype(BF16)

    value_part(3)
    to_core(0, 0, 3)
    value_part(1)
    to_chip(0)
    z_start(O, NEAR)
    value_part(2)
    to_core(0, 1, 2)
    value_part(0)
    ins[...] = jnp.sum(ot[0] * wide(gt[...]), axis=0, keepdims=True)
    second(3)
    to_core(1, 0, 3)
    total(0, (0,))
    second(1)
    to_chip(1)
    total(0, (1,))
    second(2)
    to_core(1, 1, 2)
    second(0)
    dqb[...] = (dqt[...] * FACTOR).astype(BF16).T
    z_start(DQ)
    total(1)
    for copies in xc + yc:
        for copy in copies:
            copy.wait_send()
    for a in range(8):
        z_sent(a)
        if a >= 4:
            z_arrive(a)


def fused(starts, q, k, v, g):
    out = jax.ShapeDtypeStruct((TOK, HEADS * D), BF16)
    anyspace = pl.BlockSpec(memory_space=pl.ANY)
    dma = pltpu.SemaphoreType.DMA
    return pl.pallas_call(
        fused_kernel,
        out_shape=(out,) * 4,
        in_specs=[pl.BlockSpec(memory_space=pltpu.SMEM)] + [anyspace] * 4,
        out_specs=[anyspace] * 4,
        scratch_shapes=[
            pltpu.VMEM((COL, D), BF16),
            pltpu.VMEM((COL, D), BF16),
            pltpu.VMEM((NX, COL, D), BF16),
            pltpu.VMEM((NX, COL, D), BF16),
            pltpu.VMEM((2 * D, COL), BF16),
            pltpu.VMEM((D, COL), BF16),
            pltpu.VMEM((NX, D, COL), BF16),
            pltpu.VMEM((NX, D, COL), BF16),
            pltpu.VMEM((NX, COL, COL), BF16),
            pltpu.VMEM((NX, D, COL), F32),
            pltpu.VMEM((NX, 1, COL), F32),
            pltpu.VMEM((NX, 1, COL), F32),
            pltpu.VMEM((NX, COL, D), BF16),
            pltpu.VMEM((NX, 1, COL), F32),
            pltpu.VMEM((1, COL), F32),
            pltpu.VMEM((D, COL), F32),
            pltpu.VMEM((2, COL, QB), F32),
            pltpu.VMEM((2, NX, COL, D), BF16),
            pltpu.VMEM((2, 3, COL, D), BF16),
            pltpu.VMEM((2, COL, D), BF16),
            pltpu.VMEM((2, COL, D), BF16),
            pltpu.VMEM((COL, D), BF16),
            pltpu.VMEM((COL, D), BF16),
            dma((8, 2)),
            dma((8, 2)),
            dma((2, 3)),
            dma((2, 3)),
            dma((2, 4)),
            dma((2, 4)),
        ],
        compiler_params=pltpu.CompilerParams(
            collective_id=0, has_side_effects=True, vmem_limit_bytes=58 * 1024 * 1024
        ),
        name="fused",
    )(starts, q, k, v, g)


def handed_on_kernel(*refs):
    given, taken, (held, come, gone) = refs[:4], refs[4:8], refs[8:]
    into = [pltpu.make_async_copy(given[n], held.at[n], come.at[n]) for n in range(4)]
    out = [pltpu.make_async_copy(held.at[n], taken[n], gone.at[n]) for n in range(4)]
    for copy in into:
        copy.start()
    for n in range(4):
        into[n].wait()
        out[n].start()
    for copy in out:
        copy.wait()


def handed_on(*arrays):
    anyspace = pl.BlockSpec(memory_space=pl.ANY)
    return pl.pallas_call(
        handed_on_kernel,
        out_shape=tuple(jax.ShapeDtypeStruct(a.shape, a.dtype) for a in arrays),
        in_specs=[anyspace] * 4,
        out_specs=[anyspace] * 4,
        scratch_shapes=[
            pltpu.VMEM((4,) + arrays[0].shape, arrays[0].dtype),
            pltpu.SemaphoreType.DMA((4,)),
            pltpu.SemaphoreType.DMA((4,)),
        ],
        compiler_params=pltpu.CompilerParams(vmem_limit_bytes=58 * 1024 * 1024),
        name="handed_on",
    )(*arrays)


def per_device(queries, key_rows, value_rows, out_cotangent, scale_starts):
    attended, query_grad, value_grad, key_grad = fused(scale_starts, queries, key_rows, value_rows, out_cotangent)
    return handed_on(attended, query_grad, key_grad, value_grad)


def solution(mesh):
    rows = P(("dp", "seq"), None)
    return jax.shard_map(
        per_device,
        mesh=mesh,
        in_specs=(rows, rows, rows, rows, P("dp")),
        out_specs=(rows,) * 4,
        check_vma=False,
    )
```
